32 devices in a mesh: grp: 2 (over y), row: 4 (over x, core), col: 4 (over z).
Axes of the slice: x: 2, y: 2, z: 4, core: 2. Of those that a mesh axis runs over, the one named last changes fastest.
Arguments:
- grad_out: bfloat16 [512, 8192], P(('grp', 'row'), 'col'), parts along dimension 0, may hold values from -6 to 6
- activations: bfloat16 [512, 28672], P(('grp', 'col'), 'row'), parts along dimension 0, may hold values from -6 to 6
- weight_blocks: bfloat16 [4, 4, 537, 128, 128], P('row', 'col'), may hold values from -0.0625 to 0.0625
- block_ids: int32 [4, 4, 537], P('row', 'col'), may hold values from 0 to 895, as said below
- block_counts: int32 [4, 4], P('row', 'col'), may hold values from 179 to 537, as said below
Outputs:
- grad_hidden: bfloat16 [512, 28672], P(('grp', 'col'), 'row'), parts along dimension 0
- grad_weight: bfloat16 [8, 4, 537, 128, 128], P(('grp', 'row'), 'col'), parts along dimension 0
The draws below stay inside these ranges and needn't reach their ends.
There are 2 independent parts, one for each index of `grp`. The reference program is written for one: setup_inputs(seed, part) draws one part's arguments, and reference() takes and returns one part's arrays. A program takes and returns all parts, laid end to end along the dimension named above; an argument that names none is the same for every part. Nothing has to cross between parts.
Inputs may be any that keep to these rules, and one draw needn't show every extreme that they name: `block_ids`: within one shard the 537 entries are distinct block numbers. `block_counts`: some shard has all 537 slots live in every draw.
All inputs are finite; a program needn't handle non-finite values.
Results may differ from the reference program's by a relative error of at most 0.009.
Values may be sent and summed in bfloat16 or wider, within the bound.
No kernel may reach another device: no remote copies, remote signals or barrier semaphores. Data moves between devices by JAX's collectives and lax.ppermute only.
A program may use at most 448 MiB of HBM per device.

```python
import jax
import jax.numpy as jnp
from jax import lax

D = 8192
FF = 28672
BLOCK = 128
TOKENS = 256
SHARDS_R = 4
SHARDS_C = 4
ROW_BLOCKS = 56
COL_BLOCKS = 16
SHARD_BLOCKS = 896
MOST_KEPT = 537
LEAST_KEPT = 179


def draw_block_ids(key, part):
    key = jax.random.fold_in(key, 11)
    keys = jax.random.split(key, SHARDS_R * SHARDS_C)
    orders = jax.vmap(lambda k: jax.random.permutation(k, SHARD_BLOCKS))(keys)
    return orders[:, :MOST_KEPT].reshape(SHARDS_R, SHARDS_C, MOST_KEPT).astype(jnp.int32)


def draw_block_counts(key, part):
    key = jax.random.fold_in(key, 23)
    first, second = jax.random.split(key)
    counts = jax.random.randint(first, (SHARDS_R * SHARDS_C,), LEAST_KEPT, MOST_KEPT + 1)
    fullest = jax.random.randint(second, (), 0, SHARDS_R * SHARDS_C)
    counts = counts.at[fullest].set(MOST_KEPT)
    return counts.reshape(SHARDS_R, SHARDS_C).astype(jnp.int32)


def block_levels(key, shape, pieces, low, high):
    def one(dim, shards_of):
        draws = jax.random.uniform(jax.random.fold_in(jax.random.fold_in(key, 6), dim), (shards_of,), jnp.float32, low / len(pieces), high / len(pieces))
        return jnp.repeat(jnp.exp(draws), shape[dim] // shards_of).reshape((-1,) + (1,) * (len(shape) - dim - 1))

    loudness = one(*pieces[0])
    for cut in pieces[1:]:
        loudness = loudness * one(*cut)
    return loudness


def gaussian(own_key, shape, width, bound, cuts=(), kind=jnp.bfloat16):
    drawn = jax.random.normal(own_key, shape, jnp.float32) * width
    if len(cuts) > 0:
        drawn = block_levels(own_key, shape, cuts, -0.22, 0.18) * drawn
    return jnp.clip(drawn, min=-bound, max=bound).astype(kind)


def setup_inputs(seed: int = 0, part: int = 0) -> dict:
    key_of = jax.random.split(jax.random.key(seed), 6)
    own_keys = jax.random.split(jax.random.fold_in(key_of[5], part), 6)
    return {
        "grad_out": gaussian(own_keys[0], (TOKENS, D), 1.0, 6.0, ((0, 4), (1, 4))),
        "activations": gaussian(own_keys[1], (TOKENS, FF), 1.0, 6.0, ((0, 4), (1, 4))),
        "weight_blocks": gaussian(key_of[2], (SHARDS_R, SHARDS_C, MOST_KEPT, BLOCK, BLOCK), D ** -0.5, 0.0625, ((0, 4), (1, 4))),
        "block_ids": draw_block_ids(jax.random.fold_in(key_of[5], 71), part),
        "block_counts": draw_block_counts(jax.random.fold_in(key_of[5], 71), part),
    }


def shard_terms(grad_out, activations, weights, ids, count, r, c):
    cols = lax.dynamic_slice_in_dim(grad_out, c * (COL_BLOCKS * BLOCK), COL_BLOCKS * BLOCK, 1)
    cols = cols.reshape(TOKENS, COL_BLOCKS, BLOCK)
    rows = lax.dynamic_slice_in_dim(activations, r * (ROW_BLOCKS * BLOCK), ROW_BLOCKS * BLOCK, 1)
    rows = rows.reshape(TOKENS, ROW_BLOCKS, BLOCK)
    brow = (ids // COL_BLOCKS).astype(jnp.int32)
    bcol = (ids % COL_BLOCKS).astype(jnp.int32)
    live = jnp.arange(MOST_KEPT, dtype=jnp.int32) < count
    kept = jnp.where(live[:, None, None], weights, jnp.zeros_like(weights)).astype(jnp.float32)
    dsel = jnp.take(cols, bcol, axis=1).astype(jnp.float32)
    hsel = jnp.take(rows, brow, axis=1).astype(jnp.float32)
    prod = jnp.einsum("tsj,sij->tsi", dsel, kept, precision=lax.Precision.HIGHEST)
    part = jnp.zeros((TOKENS, ROW_BLOCKS, BLOCK), jnp.float32).at[:, brow].add(prod)
    part = lax.optimization_barrier(part.astype(jnp.bfloat16)).astype(jnp.float32)
    grad = jnp.einsum("tsi,tsj->sij", hsel, dsel, precision=lax.Precision.HIGHEST)
    grad = jnp.where(live[:, None, None], grad, jnp.zeros_like(grad)).astype(jnp.bfloat16)
    return part, grad


def reference(grad_out, activations, weight_blocks, block_ids, block_counts):
    def per_row(r):
        def per_col(total, c):
            part, grad = shard_terms(grad_out, activations, weight_blocks[r, c], block_ids[r, c], block_counts[r, c], r, c)
            return total + part, grad

        start = jnp.zeros((TOKENS, ROW_BLOCKS, BLOCK), jnp.float32)
        total, grads = lax.scan(per_col, start, jnp.arange(SHARDS_C, dtype=jnp.int32))
        return total.astype(jnp.bfloat16).reshape(TOKENS, ROW_BLOCKS * BLOCK), grads

    hidden_rows, grad_weight = lax.map(per_row, jnp.arange(SHARDS_R, dtype=jnp.int32))
    grad_hidden = jnp.transpose(hidden_rows, (1, 0, 2)).reshape(TOKENS, FF)
    return grad_hidden, grad_weight
```

```python
import functools

import jax
import jax.numpy as jnp
from jax import lax
from jax.experimental import pallas as pl
from jax.experimental.pallas import tpu as pltpu
from jax.sharding import PartitionSpec as P

BLOCK = 128
CHUNKS = 2
MIB = 1 << 20
SMEM = pl.BlockSpec(memory_space=pltpu.SMEM)
VMEM = pl.BlockSpec(memory_space=pltpu.VMEM)
ANY = pl.BlockSpec(memory_space=pl.ANY)


def partial_body(chunk, tile, slot_of, grads, blocks, out):
    cols, high = grads.shape[1] // BLOCK, tile // BLOCK

    def block(r, c):
        slot = slot_of[(chunk * (out.shape[1] // BLOCK) + r) * cols + c]
        held = blocks[jnp.maximum(slot, 0)]
        return jnp.where(slot >= 0, held, jnp.zeros_like(held))

    def step(i, carry):
        weights = jnp.concatenate(
            [jnp.concatenate([block(i * high + p, c) for c in range(cols)], 1) for p in range(high)], 0
        )
        out[:, pl.ds(pl.multiple_of(i * tile, tile), tile)] = lax.dot_general(
            grads[...], weights, (((1,), (1,)), ((), ())), preferred_element_type=jnp.float32
        ).astype(out.dtype)
        return carry

    lax.fori_loop(0, out.shape[1] // tile, step, 0)


def first_partial_kernel(tile, masks, slot_of, me, *refs):
    pieces, (blocks, out, grads) = refs[: len(masks)], refs[len(masks) :]
    rows = pieces[0].shape[0]
    for mask, piece in zip(masks, pieces):
        at = pl.multiple_of((me[0] ^ mask) * rows, rows)
        grads[pl.ds(at, rows), :] = piece[...]
    partial_body(0, tile, slot_of, grads, blocks, out)


def partial_kernel(chunk, tile, slot_of, grads, blocks, out):
    partial_body(chunk, tile, slot_of, grads, blocks, out)


def weight_grad_kernel(chunk, tile, n, slot_of, where, count, own, grads, *refs):
    flows = refs[: n - 1], refs[n - 1 : 2 * n - 2]
    refs = refs[2 * n - 2 :]
    if chunk:
        refs = refs[1:]
    out, done, acts, dense, zero, act_sem, sem = refs
    me = where[0]
    rows, cols = dense.shape[0], dense.shape[1]
    part, width = acts.shape[0] // n, acts.shape[1]

    def spot(i):
        return acts.at[pl.ds(pl.multiple_of(i * part, part), part), :]

    copies = [(None, pltpu.make_async_copy(own.at[:, pl.ds(chunk * width, width)], spot(me), act_sem))]
    for e, flow in enumerate(flows):
        from_left = (me + e) % 2 == 1
        for j in range(n - 1):
            owner = jnp.where(from_left, me - 1 - j, me + 1 + j)
            needed = (owner >= 0) & (owner < n)
            copies.append((needed, pltpu.make_async_copy(flow[j], spot(jnp.clip(owner, 0, n - 1)), act_sem)))
    for method in ("start", "wait"):
        for needed, copy in copies:
            if needed is None:
                getattr(copy, method)()
            else:
                pl.when(needed)(getattr(copy, method))
        if method == "start" and chunk == 0:
            zero[...] = jnp.zeros_like(zero)

            def clear(slot, carry):
                pltpu.make_async_copy(zero, out.at[slot], sem).start()
                return carry

            lax.fori_loop(count[0], out.shape[0], clear, 0)

    wide = min(512, grads.shape[1])

    def step(i, live):
        turned = acts[:, pl.ds(pl.multiple_of(i * tile, tile), tile)].T
        for j in range(0, grads.shape[1], wide):
            product = jnp.dot(turned, grads[:, j : j + wide], preferred_element_type=jnp.float32).astype(dense.dtype)
            for p in range(tile // BLOCK):
                for q in range(wide // BLOCK):
                    dense[i * (tile // BLOCK) + p, j // BLOCK + q] = product[
                        p * BLOCK : (p + 1) * BLOCK, q * BLOCK : (q + 1) * BLOCK
                    ]
        for p in range(tile // BLOCK):
            for c in range(cols):
                r = i * (tile // BLOCK) + p
                slot = slot_of[(chunk * rows + r) * cols + c]

                @pl.when(slot >= 0)
                def _():
                    pltpu.make_async_copy(dense.at[r, c], out.at[slot], sem).start()

                live = live + (slot >= 0).astype(jnp.int32)
        return live

    live = lax.fori_loop(0, rows * BLOCK // tile, step, jnp.int32(0))
    if chunk == 0:
        live = live + out.shape[0] - count[0]

    def drain(i, carry):
        pltpu.make_async_copy(dense.at[0, 0], out.at[0], sem).wait()
        return carry

    lax.fori_loop(0, live, drain, 0)
    done[0] = live


def params(mib):
    return pltpu.CompilerParams(vmem_limit_bytes=mib * MIB)


def cost(flops, moved):
    return pl.CostEstimate(flops=flops, bytes_accessed=moved, transcendentals=0)


def shards(grad_out, activations, weight_blocks, block_ids, block_counts):
    R, n = lax.axis_size("row"), lax.axis_size("col")
    r, c = lax.axis_index("row"), lax.axis_index("col")
    rows_g, depth = grad_out.shape
    part, hidden = activations.shape
    tokens = n * part
    width = hidden // CHUNKS
    col_blocks, row_blocks = depth // BLOCK, hidden // BLOCK
    tile = width // 2 if width % (2 * BLOCK) == 0 else width
    slots = block_ids.shape[-1]
    kind = grad_out.dtype
    first = [(i, i ^ 1) for i in range(n)]
    second = [(i, i + 1) for i in range(1, n - 1, 2)] + [(i + 1, i) for i in range(1, n - 1, 2)]
    links = (first, second)
    even = c % 2 == 0
    right_going = (even, jnp.logical_not(even))
    origin = [jnp.where(goes, c, n - 1 - c) for goes in right_going]

    ids, count = block_ids[0, 0], block_counts[0]
    number = jnp.arange(slots, dtype=jnp.int32)
    held = (ids[:, None] == jnp.arange(row_blocks * col_blocks, dtype=jnp.int32)) & (number < count)[:, None]
    slot_of = jnp.max(jnp.where(held, number[:, None], -1), axis=0)

    pieces, masks = [grad_out], [0]
    bit = R // 2
    while bit:
        pairs = [(i, i ^ bit) for i in range(R)]
        pieces = pieces + [lax.ppermute(piece, "row", pairs) for piece in pieces]
        masks = masks + [mask ^ bit for mask in masks]
        bit //= 2

    blocks = weight_blocks[0, 0]
    work = cost(2 * tokens * width * depth, 2 * width * depth)
    sums, grads = pl.pallas_call(
        functools.partial(first_partial_kernel, tile, masks),
        out_shape=[jax.ShapeDtypeStruct((tokens, width), kind), jax.ShapeDtypeStruct((tokens, depth), kind)],
        in_specs=[SMEM, SMEM] + [VMEM] * (R + 1),
        out_specs=[VMEM, VMEM],
        compiler_params=params(16),
        cost_estimate=work,
        name="partial0",
    )(slot_of, r[None].astype(jnp.int32), *pieces, blocks)
    partial = [sums]

    def add_partial(h, slot_of):
        partial.append(
            pl.pallas_call(
                functools.partial(partial_kernel, h, tile),
                out_shape=jax.ShapeDtypeStruct((tokens, width), kind),
                in_specs=[SMEM, VMEM, VMEM],
                out_specs=VMEM,
                compiler_params=params(16),
                cost_estimate=work,
                name=f"partial{h}",
            )(slot_of, grads, blocks)
        )

    def rows_of(h, d):
        return lax.dynamic_slice_in_dim(partial[h], jnp.clip(d, 0, n - 1) * part, part, 0)

    def weight_grad(h, slot_of, out):
        flows = [came[h][e][j] for e in range(2) for j in range(n - 1)]
        given = [slot_of, c[None].astype(jnp.int32), count, activations, grads, *flows]
        specs = [SMEM, SMEM, SMEM, ANY, VMEM] + [ANY] * (2 * n - 2)
        if h:
            given.append(out)
            specs.append(ANY)
        return pl.pallas_call(
            functools.partial(weight_grad_kernel, h, tile, n),
            out_shape=[jax.ShapeDtypeStruct((slots, BLOCK, BLOCK), kind), jax.ShapeDtypeStruct((1,), jnp.int32)],
            in_specs=specs,
            out_specs=[ANY, SMEM],
            scratch_shapes=[
                pltpu.VMEM((tokens, width), kind),
                pltpu.VMEM((row_blocks // CHUNKS, col_blocks, BLOCK, BLOCK), kind),
                pltpu.VMEM((BLOCK, BLOCK), kind),
                pltpu.SemaphoreType.DMA,
                pltpu.SemaphoreType.DMA,
            ],
            input_output_aliases={len(given) - 1: 0} if h else {},
            compiler_params=params(20),
            cost_estimate=cost(2 * tokens * width * depth, 2 * weight_blocks.size // CHUNKS),
            name=f"weight_grad{h}",
        )(*given)

    came = [[[] for _ in links] for _ in range(CHUNKS)]
    out = done = None
    for k in range(n):
        for h in range(CHUNKS):
            messages = []
            for e in range(len(links)):
                if k == 0:
                    message = activations[:, h * width : (h + 1) * width]
                else:
                    last = came[h][1 - e][k - 1]
                    if done is not None:
                        last, _ = lax.optimization_barrier((last, done))
                    d = jnp.where(right_going[e], n - k + origin[e], k - 1 - origin[e])
                    message = jnp.where(
                        k <= origin[e], last, rows_of(h, d) + jnp.where(origin[e] > 0, last, jnp.zeros_like(last))
                    )
                messages.append(message)
            for e, pairs in enumerate(links):
                came[h][e].append(lax.ppermute(messages[e], "col", pairs))
            after, _ = lax.optimization_barrier((slot_of, messages))
            if k == 1 and h + 1 < CHUNKS:
                add_partial(h + 1, after)
            if k == n - 1:
                out, done = weight_grad(h, after, out)

    hidden_parts = []
    inner = (c > 0) & (c < n - 1)
    for h in range(CHUNKS):
        mine, _ = lax.optimization_barrier((rows_of(h, c), done))
        total = mine.astype(jnp.float32) + came[h][0][n - 1].astype(jnp.float32)
        total = total + jnp.where(inner, came[h][1][n - 1], jnp.zeros_like(came[h][1][n - 1])).astype(jnp.float32)
        hidden_parts.append(total.astype(kind))
    return jnp.concatenate(hidden_parts, 1), out[None, None]


def solution(mesh):
    placed = (
        P(("grp", "row"), "col"),
        P(("grp", "col"), "row"),
        P("row", "col", None, None, None),
        P("row", "col", None),
        P("row", "col"),
    )
    return jax.shard_map(
        shards,
        mesh=mesh,
        in_specs=placed,
        out_specs=(P(("grp", "col"), "row"), P(("grp", "row"), "col", None, None, None)),
        check_vma=False,
    )
```

```python
import functools

import jax
import jax.numpy as jnp
from jax import lax
from jax.experimental import pallas as pl
from jax.experimental.pallas import tpu as pltpu
from jax.sharding import PartitionSpec as P

BLOCK = 128
CHUNKS = 2
MIB = 1 << 20
SMEM = pl.BlockSpec(memory_space=pltpu.SMEM)
VMEM = pl.BlockSpec(memory_space=pltpu.VMEM)
ANY = pl.BlockSpec(memory_space=pl.ANY)


def partial_body(chunk, tile, slot_of, grads, blocks, out):
    cols, high = grads.shape[1] // BLOCK, tile // BLOCK

    def block(r, c):
        slot = slot_of[(chunk * (out.shape[1] // BLOCK) + r) * cols + c]
        held = blocks[jnp.maximum(slot, 0)]
        return jnp.where(slot >= 0, held, jnp.zeros_like(held))

    def step(i, carry):
        weights = jnp.concatenate(
            [jnp.concatenate([block(i * high + p, c) for c in range(cols)], 1) for p in range(high)], 0
        )
        out[:, pl.ds(pl.multiple_of(i * tile, tile), tile)] = lax.dot_general(
            grads[...], weights, (((1,), (1,)), ((), ())), preferred_element_type=jnp.float32
        ).astype(out.dtype)
        return carry

    lax.fori_loop(0, out.shape[1] // tile, step, 0)


def first_partial_kernel(tile, masks, slot_of, me, *refs):
    pieces, (blocks, out, grads, sems) = refs[: len(masks)], refs[len(masks) :]
    rows = pieces[0].shape[0]
    copies = []
    for i, (mask, piece) in enumerate(zip(masks, pieces)):
        at = pl.multiple_of((me[0] ^ mask) * rows, rows)
        copies.append(pltpu.make_async_copy(piece, grads.at[pl.ds(at, rows), :], sems.at[i]))
    for copy in copies:
        copy.start()
    for copy in copies:
        copy.wait()
    partial_body(0, tile, slot_of, grads, blocks, out)


def partial_kernel(chunk, tile, slot_of, grads, blocks, out):
    partial_body(chunk, tile, slot_of, grads, blocks, out)


def weight_grad_kernel(chunk, tile, n, slot_of, where, count, own, grads, *refs):
    flows = refs[: n - 1], refs[n - 1 : 2 * n - 2]
    refs = refs[2 * n - 2 :]
    out, done, acts, dense, zero, act_sem, sem = refs[-7:]
    me = where[0]
    rows, cols = dense.shape[0], dense.shape[1]
    part, width = acts.shape[0] // n, acts.shape[1]

    def spot(i):
        return acts.at[pl.ds(pl.multiple_of(i * part, part), part), :]

    copies = [(None, pltpu.make_async_copy(own.at[:, pl.ds(chunk * width, width)], spot(me), act_sem))]
    for e, flow in enumerate(flows):
        from_left = (me + e) % 2 == 1
        for j in range(n - 1):
            owner = jnp.where(from_left, me - 1 - j, me + 1 + j)
            needed = (owner >= 0) & (owner < n)
            copies.append((needed, pltpu.make_async_copy(flow[j], spot(jnp.clip(owner, 0, n - 1)), act_sem)))
    for method in ("start", "wait"):
        for needed, copy in copies:
            if needed is None:
                getattr(copy, method)()
            else:
                pl.when(needed)(getattr(copy, method))
        if method == "start" and chunk == 0:
            zero[...] = jnp.zeros_like(zero)

            group = zero.shape[0]
            groups = (out.shape[0] - count[0]) // group

            @pl.loop(0, groups)
            def _(i):
                pltpu.make_async_copy(zero, out.at[pl.ds(count[0] + i * group, group)], sem).start()

            @pl.loop(count[0] + groups * group, out.shape[0])
            def _(slot):
                pltpu.make_async_copy(zero.at[0], out.at[slot], sem).start()

    wide = min(512, grads.shape[1])

    def step(i, live):
        turned = acts[:, pl.ds(pl.multiple_of(i * tile, tile), tile)].T
        for j in range(0, grads.shape[1], wide):
            product = jnp.dot(turned, grads[:, j : j + wide], preferred_element_type=jnp.float32).astype(dense.dtype)
            for p in range(tile // BLOCK):
                for q in range(wide // BLOCK):
                    dense[i * (tile // BLOCK) + p, j // BLOCK + q] = product[
                        p * BLOCK : (p + 1) * BLOCK, q * BLOCK : (q + 1) * BLOCK
                    ]
        for p in range(tile // BLOCK):
            for c in range(cols):
                r = i * (tile // BLOCK) + p
                slot = slot_of[(chunk * rows + r) * cols + c]

                @pl.when(slot >= 0)
                def _():
                    pltpu.make_async_copy(dense.at[r, c], out.at[slot], sem).start()

                live = live + (slot >= 0).astype(jnp.int32)
        return live

    live = lax.fori_loop(0, rows * BLOCK // tile, step, jnp.int32(0))
    if chunk == 0:
        live = live + out.shape[0] - count[0]

    def drain(i, carry):
        pltpu.make_async_copy(dense.at[0, 0], out.at[0], sem).wait()
        return carry

    lax.fori_loop(0, live, drain, 0)
    done[0] = live


def params(mib):
    return pltpu.CompilerParams(vmem_limit_bytes=mib * MIB)


def cost(flops, moved):
    return pl.CostEstimate(flops=flops, bytes_accessed=moved, transcendentals=0)


def shards(grad_out, activations, weight_blocks, block_ids, block_counts):
    R, n = lax.axis_size("row"), lax.axis_size("col")
    r, c = lax.axis_index("row"), lax.axis_index("col")
    rows_g, depth = grad_out.shape
    part, hidden = activations.shape
    tokens = n * part
    width = hidden // CHUNKS
    col_blocks, row_blocks = depth // BLOCK, hidden // BLOCK
    tile = width // 2 if width % (2 * BLOCK) == 0 else width
    slots = block_ids.shape[-1]
    kind = grad_out.dtype
    first = [(i, i ^ 1) for i in range(n)]
    second = [(i, i + 1) for i in range(1, n - 1, 2)] + [(i + 1, i) for i in range(1, n - 1, 2)]
    links = (first, second)
    even = c % 2 == 0
    right_going = (even, jnp.logical_not(even))
    origin = [jnp.where(goes, c, n - 1 - c) for goes in right_going]

    ids, count = block_ids[0, 0], block_counts[0]
    number = jnp.arange(slots, dtype=jnp.int32)
    held = (ids[:, None] == jnp.arange(row_blocks * col_blocks, dtype=jnp.int32)) & (number < count)[:, None]
    slot_of = jnp.max(jnp.where(held, number[:, None], -1), axis=0)

    pieces, masks = [grad_out], [0]
    bit = R // 2
    while bit:
        pairs = [(i, i ^ bit) for i in range(R)]
        pieces = pieces + [lax.ppermute(piece, "row", pairs) for piece in pieces]
        masks = masks + [mask ^ bit for mask in masks]
        bit //= 2

    blocks = weight_blocks[0, 0]
    work = cost(2 * tokens * width * depth, 2 * width * depth)
    sums, grads = pl.pallas_call(
        functools.partial(first_partial_kernel, tile, masks),
        out_shape=[jax.ShapeDtypeStruct((tokens, width), kind), jax.ShapeDtypeStruct((tokens, depth), kind)],
        in_specs=[SMEM, SMEM] + [ANY] * R + [VMEM],
        out_specs=[VMEM, VMEM],
        scratch_shapes=[pltpu.SemaphoreType.DMA((R,))],
        compiler_params=params(16),
        cost_estimate=work,
        name="partial0",
    )(slot_of, r[None].astype(jnp.int32), *pieces, blocks)
    partial = [sums]

    def add_partial(h, slot_of):
        partial.append(
            pl.pallas_call(
                functools.partial(partial_kernel, h, tile),
                out_shape=jax.ShapeDtypeStruct((tokens, width), kind),
                in_specs=[SMEM, VMEM, VMEM],
                out_specs=VMEM,
                compiler_params=params(16),
                cost_estimate=work,
                name=f"partial{h}",
            )(slot_of, grads, blocks)
        )

    def rows_of(h, d):
        return lax.dynamic_slice_in_dim(partial[h], jnp.clip(d, 0, n - 1) * part, part, 0)

    def weight_grad(h, messages, out):
        flows = [came[h][e][j] for e in range(2) for j in range(n - 1)]
        given = [slot_of, c[None].astype(jnp.int32), count, activations, grads, *flows]
        given += messages
        specs = [SMEM, SMEM, SMEM, ANY, VMEM] + [ANY] * (2 * n - 2 + len(messages))
        if h:
            given.append(out)
            specs.append(ANY)
        return pl.pallas_call(
            functools.partial(weight_grad_kernel, h, tile, n),
            out_shape=[jax.ShapeDtypeStruct((slots, BLOCK, BLOCK), kind), jax.ShapeDtypeStruct((1,), jnp.int32)],
            in_specs=specs,
            out_specs=[ANY, SMEM],
            scratch_shapes=[
                pltpu.VMEM((tokens, width), kind),
                pltpu.VMEM((row_blocks // CHUNKS, col_blocks, BLOCK, BLOCK), kind),
                pltpu.VMEM((8, BLOCK, BLOCK), kind),
                pltpu.SemaphoreType.DMA,
                pltpu.SemaphoreType.DMA,
            ],
            input_output_aliases={len(given) - 1: 0} if h else {},
            compiler_params=params(20),
            cost_estimate=cost(2 * tokens * width * depth, 2 * weight_blocks.size // CHUNKS),
            name=f"weight_grad{h}",
        )(*given)

    came = [[[] for _ in links] for _ in range(CHUNKS)]
    out = done = None
    for k in range(n):
        for h in range(CHUNKS):
            messages = []
            for e in range(len(links)):
                if k == 0:
                    message = activations[:, h * width : (h + 1) * width]
                else:
                    last = came[h][1 - e][k - 1]
                    if done is not None:
                        last, _ = lax.optimization_barrier((last, done))
                    d = jnp.where(right_going[e], n - k + origin[e], k - 1 - origin[e])
                    message = jnp.where(
                        k <= origin[e], last, rows_of(h, d) + jnp.where(origin[e] > 0, last, jnp.zeros_like(last))
                    )
                messages.append(message)
            for e, pairs in enumerate(links):
                came[h][e].append(lax.ppermute(messages[e], "col", pairs))
            after, _ = lax.optimization_barrier((slot_of, messages))
            if k == 1 and h + 1 < CHUNKS:
                add_partial(h + 1, after)
            if k == n - 1:
                out, done = weight_grad(h, messages, out)

    hidden_parts = []
    inner = (c > 0) & (c < n - 1)
    for h in range(CHUNKS):
        mine, _ = lax.optimization_barrier((rows_of(h, c), done))
        total = mine.astype(jnp.float32) + came[h][0][n - 1].astype(jnp.float32)
        total = total + jnp.where(inner, came[h][1][n - 1], jnp.zeros_like(came[h][1][n - 1])).astype(jnp.float32)
        hidden_parts.append(total.astype(kind))
    return jnp.concatenate(hidden_parts, 1), out[None, None]


def solution(mesh):
    placed = (
        P(("grp", "row"), "col"),
        P(("grp", "col"), "row"),
        P("row", "col", None, None, None),
        P("row", "col", None),
        P("row", "col"),
    )
    return jax.shard_map(
        shards,
        mesh=mesh,
        in_specs=placed,
        out_specs=(P(("grp", "col"), "row"), P(("grp", "row"), "col", None, None, None)),
        check_vma=False,
    )
```

```python
import functools

import jax
import jax.numpy as jnp
from jax import lax
from jax.experimental import pallas as pl
from jax.experimental.pallas import tpu as pltpu
from jax.sharding import PartitionSpec as P

BLOCK = 128
CHUNKS = 2
MIB = 1 << 20
SMEM = pl.BlockSpec(memory_space=pltpu.SMEM)
VMEM = pl.BlockSpec(memory_space=pltpu.VMEM)
ANY = pl.BlockSpec(memory_space=pl.ANY)


def partial_body(chunk, tile, slot_of, grads, blocks, out):
    cols, high = grads.shape[1] // BLOCK, tile // BLOCK

    def block(r, c):
        slot = slot_of[(chunk * (out.shape[1] // BLOCK) + r) * cols + c]
        held = blocks[jnp.maximum(slot, 0)]
        return jnp.where(slot >= 0, held, jnp.zeros_like(held))

    def step(i, carry):
        weights = jnp.concatenate(
            [jnp.concatenate([block(i * high + p, c) for c in range(cols)], 1) for p in range(high)], 0
        )
        out[:, pl.ds(pl.multiple_of(i * tile, tile), tile)] = lax.dot_general(
            grads[...], weights, (((1,), (1,)), ((), ())), preferred_element_type=jnp.float32
        ).astype(out.dtype)
        return carry

    lax.fori_loop(0, out.shape[1] // tile, step, 0)


def first_partial_kernel(tile, masks, slot_of, me, *refs):
    pieces, (blocks, out, grads, sems) = refs[: len(masks)], refs[len(masks) :]
    rows = pieces[0].shape[0]
    copies = []
    for i, (mask, piece) in enumerate(zip(masks, pieces)):
        at = pl.multiple_of((me[0] ^ mask) * rows, rows)
        copies.append(pltpu.make_async_copy(piece, grads.at[pl.ds(at, rows), :], sems.at[i]))
    for copy in copies:
        copy.start()
    for copy in copies:
        copy.wait()
    partial_body(0, tile, slot_of, grads, blocks, out)


def partial_kernel(chunk, tile, slot_of, grads, blocks, out):
    partial_body(chunk, tile, slot_of, grads, blocks, out)


def weight_grad_kernel(chunk, tile, n, slot_of, where, count, own, grads, *refs):
    flows = refs[: n - 1], refs[n - 1 : 2 * n - 2]
    refs = refs[2 * n - 2 :]
    out, done, acts, dense, zero, act_sem, sem = refs[-7:]
    me = where[0]
    rows, cols = dense.shape[0], dense.shape[1]
    part, width = acts.shape[0] // n, acts.shape[1]

    def spot(i):
        return acts.at[pl.ds(pl.multiple_of(i * part, part), part), :]

    copies = [(None, pltpu.make_async_copy(own.at[:, pl.ds(chunk * width, width)], spot(me), act_sem))]
    for e, flow in enumerate(flows):
        from_left = (me + e) % 2 == 1
        for j in range(n - 1):
            owner = jnp.where(from_left, me - 1 - j, me + 1 + j)
            needed = (owner >= 0) & (owner < n)
            copies.append((needed, pltpu.make_async_copy(flow[j], spot(jnp.clip(owner, 0, n - 1)), act_sem)))
    for method in ("start", "wait"):
        for needed, copy in copies:
            if needed is None:
                getattr(copy, method)()
            else:
                pl.when(needed)(getattr(copy, method))
        if method == "start" and chunk == CHUNKS - 1:
            zero[...] = jnp.zeros_like(zero)

            group = zero.shape[0]
            groups = (out.shape[0] - count[0]) // group

            @pl.loop(0, groups)
            def _(i):
                pltpu.make_async_copy(zero, out.at[pl.ds(count[0] + i * group, group)], sem).start()

            @pl.loop(count[0] + groups * group, out.shape[0])
            def _(slot):
                pltpu.make_async_copy(zero.at[0], out.at[slot], sem).start()

    wide = min(512, grads.shape[1])

    def step(i, live):
        turned = acts[:, pl.ds(pl.multiple_of(i * tile, tile), tile)].T
        for j in range(0, grads.shape[1], wide):
            product = jnp.dot(turned, grads[:, j : j + wide], preferred_element_type=jnp.float32).astype(dense.dtype)
            for p in range(tile // BLOCK):
                for q in range(wide // BLOCK):
                    dense[i * (tile // BLOCK) + p, j // BLOCK + q] = product[
                        p * BLOCK : (p + 1) * BLOCK, q * BLOCK : (q + 1) * BLOCK
                    ]
        for p in range(tile // BLOCK):
            for c in range(cols):
                r = i * (tile // BLOCK) + p
                slot = slot_of[(chunk * rows + r) * cols + c]

                @pl.when(slot >= 0)
                def _():
                    pltpu.make_async_copy(dense.at[r, c], out.at[slot], sem).start()

                live = live + (slot >= 0).astype(jnp.int32)
        return live

    live = lax.fori_loop(0, rows * BLOCK // tile, step, jnp.int32(0))
    if chunk == CHUNKS - 1:
        live = live + out.shape[0] - count[0]

    def drain(i, carry):
        pltpu.make_async_copy(dense.at[0, 0], out.at[0], sem).wait()
        return carry

    lax.fori_loop(0, live, drain, 0)
    done[0] = live


def params(mib):
    return pltpu.CompilerParams(vmem_limit_bytes=mib * MIB)


def cost(flops, moved):
    return pl.CostEstimate(flops=flops, bytes_accessed=moved, transcendentals=0)


def shards(grad_out, activations, weight_blocks, block_ids, block_counts):
    R, n = lax.axis_size("row"), lax.axis_size("col")
    r, c = lax.axis_index("row"), lax.axis_index("col")
    rows_g, depth = grad_out.shape
    part, hidden = activations.shape
    tokens = n * part
    width = hidden // CHUNKS
    col_blocks, row_blocks = depth // BLOCK, hidden // BLOCK
    tile = width // 2 if width % (2 * BLOCK) == 0 else width
    slots = block_ids.shape[-1]
    kind = grad_out.dtype
    first = [(i, i ^ 1) for i in range(n)]
    second = [(i, i + 1) for i in range(1, n - 1, 2)] + [(i + 1, i) for i in range(1, n - 1, 2)]
    links = (first, second)
    even = c % 2 == 0
    right_going = (even, jnp.logical_not(even))
    origin = [jnp.where(goes, c, n - 1 - c) for goes in right_going]

    ids, count = block_ids[0, 0], block_counts[0]
    number = jnp.arange(slots, dtype=jnp.int32)
    held = (ids[:, None] == jnp.arange(row_blocks * col_blocks, dtype=jnp.int32)) & (number < count)[:, None]
    slot_of = jnp.max(jnp.where(held, number[:, None], -1), axis=0)

    pieces, masks = [grad_out], [0]
    bit = R // 2
    while bit:
        pairs = [(i, i ^ bit) for i in range(R)]
        pieces = pieces + [lax.ppermute(piece, "row", pairs) for piece in pieces]
        masks = masks + [mask ^ bit for mask in masks]
        bit //= 2

    blocks = weight_blocks[0, 0]
    work = cost(2 * tokens * width * depth, 2 * width * depth)
    sums, grads = pl.pallas_call(
        functools.partial(first_partial_kernel, tile, masks),
        out_shape=[jax.ShapeDtypeStruct((tokens, width), kind), jax.ShapeDtypeStruct((tokens, depth), kind)],
        in_specs=[SMEM, SMEM] + [ANY] * R + [VMEM],
        out_specs=[VMEM, VMEM],
        scratch_shapes=[pltpu.SemaphoreType.DMA((R,))],
        compiler_params=params(16),
        cost_estimate=work,
        name="partial0",
    )(slot_of, r[None].astype(jnp.int32), *pieces, blocks)
    partial = [sums]

    def add_partial(h, slot_of):
        partial.append(
            pl.pallas_call(
                functools.partial(partial_kernel, h, tile),
                out_shape=jax.ShapeDtypeStruct((tokens, width), kind),
                in_specs=[SMEM, VMEM, VMEM],
                out_specs=VMEM,
                compiler_params=params(16),
                cost_estimate=work,
                name=f"partial{h}",
            )(slot_of, grads, blocks)
        )

    def rows_of(h, d):
        return lax.dynamic_slice_in_dim(partial[h], jnp.clip(d, 0, n - 1) * part, part, 0)

    def weight_grad(h, messages, out):
        flows = [came[h][e][j] for e in range(2) for j in range(n - 1)]
        given = [slot_of, c[None].astype(jnp.int32), count, activations, grads, *flows]
        given += messages
        specs = [SMEM, SMEM, SMEM, ANY, VMEM] + [ANY] * (2 * n - 2 + len(messages))
        if h:
            given.append(out)
            specs.append(ANY)
        return pl.pallas_call(
            functools.partial(weight_grad_kernel, h, tile, n),
            out_shape=[jax.ShapeDtypeStruct((slots, BLOCK, BLOCK), kind), jax.ShapeDtypeStruct((1,), jnp.int32)],
            in_specs=specs,
            out_specs=[ANY, SMEM],
            scratch_shapes=[
                pltpu.VMEM((tokens, width), kind),
                pltpu.VMEM((row_blocks // CHUNKS, col_blocks, BLOCK, BLOCK), kind),
                pltpu.VMEM((8, BLOCK, BLOCK), kind),
                pltpu.SemaphoreType.DMA,
                pltpu.SemaphoreType.DMA,
            ],
            input_output_aliases={len(given) - 1: 0} if h else {},
            compiler_params=params(20),
            cost_estimate=cost(2 * tokens * width * depth, 2 * weight_blocks.size // CHUNKS),
            name=f"weight_grad{h}",
        )(*given)

    came = [[[] for _ in links] for _ in range(CHUNKS)]
    out = done = None
    for k in range(n):
        for h in range(CHUNKS):
            messages = []
            for e in range(len(links)):
                if k == 0:
                    message = activations[:, h * width : (h + 1) * width]
                else:
                    last = came[h][1 - e][k - 1]
                    if done is not None:
                        last, _ = lax.optimization_barrier((last, done))
                    d = jnp.where(right_going[e], n - k + origin[e], k - 1 - origin[e])
                    message = jnp.where(
                        k <= origin[e], last, rows_of(h, d) + jnp.where(origin[e] > 0, last, jnp.zeros_like(last))
                    )
                messages.append(message)
            for e, pairs in enumerate(links):
                came[h][e].append(lax.ppermute(messages[e], "col", pairs))
            after, _ = lax.optimization_barrier((slot_of, messages))
            if k == 1 and h + 1 < CHUNKS:
                add_partial(h + 1, after)
            if k == n - 1:
                out, done = weight_grad(h, messages, out)

    hidden_parts = []
    inner = (c > 0) & (c < n - 1)
    for h in range(CHUNKS):
        mine, _ = lax.optimization_barrier((rows_of(h, c), done))
        total = mine.astype(jnp.float32) + came[h][0][n - 1].astype(jnp.float32)
        total = total + jnp.where(inner, came[h][1][n - 1], jnp.zeros_like(came[h][1][n - 1])).astype(jnp.float32)
        hidden_parts.append(total.astype(kind))
    return jnp.concatenate(hidden_parts, 1), out[None, None]


def solution(mesh):
    placed = (
        P(("grp", "row"), "col"),
        P(("grp", "col"), "row"),
        P("row", "col", None, None, None),
        P("row", "col", None),
        P("row", "col"),
    )
    return jax.shard_map(
        shards,
        mesh=mesh,
        in_specs=placed,
        out_specs=(P(("grp", "col"), "row"), P(("grp", "row"), "col", None, None, None)),
        check_vma=False,
    )
```
